32 devices in a mesh: group: 2 (over x), tile: 8 (over z, y), draw: 2 (over core).
Axes of the slice: x: 2, y: 2, z: 4, core: 2. Of those that a mesh axis runs over, the one named last changes fastest.
Arguments:
- inputs: bfloat16 [4, 32, 270, 256], P(('group', 'draw'), 'tile'), parts along dimension 0, may hold values from -6 to 6
- land_mask: int32 [32, 270], P('tile'), may hold values 0 or 1
- kernel: float32 [7, 7, 256], replicated, may hold values from -0.875 to 0.875
- conv_bias: float32 [256], replicated, may hold values from -3 to 3
- norm_gain: float32 [256], replicated, may hold values from 0.1 to 1.9
- norm_bias: float32 [256], replicated, may hold values from -3 to 3
- w_in: bfloat16 [256, 1024], replicated, may hold values from -0.375 to 0.375
- b_in: float32 [1024], replicated, may hold values from -3 to 3
- w_out: bfloat16 [1024, 256], replicated, may hold values from -0.1875 to 0.1875
- b_out: float32 [256], replicated, may hold values from -3 to 3
- layer_scale: float32 [256], replicated, may hold values from 0.1 to 1.9
- cotangent: bfloat16 [4, 32, 270, 256], P(('group', 'draw'), 'tile'), parts along dimension 0, may hold values from -6 to 6
Outputs:
- output: bfloat16 [4, 32, 270, 256], P(('group', 'draw'), 'tile'), parts along dimension 0
- input_grad: bfloat16 [4, 32, 270, 256], P(('group', 'draw'), 'tile'), parts along dimension 0
- kernel_grad: float32 [14, 7, 256], P('group'), parts along dimension 0
- w_in_grad: float32 [512, 1024], P('group'), parts along dimension 0
- w_out_grad: float32 [2048, 256], P('group'), parts along dimension 0
- b_in_grad: float32 [2048], P('group'), parts along dimension 0
- channel_grads: float32 [10, 256], P('group'), parts along dimension 0
The draws below stay inside these ranges and needn't reach their ends.
There are 2 independent parts, one for each index of `group`. The reference program is written for one: setup_inputs(seed, part) draws one part's arguments, and reference() takes and returns one part's arrays. A program takes and returns all parts, laid end to end along the dimension named above; an argument that names none is the same for every part. Nothing has to cross between parts.
All inputs are finite; a program needn't handle non-finite values. No bound on the sum of `land_mask` on one device may be relied on, other than what follows from the above.
Results may differ from the reference program's by a relative error of at most 0.007.
Values may be sent and summed in bfloat16 or wider, within the bound.
A program may use at most 64 MiB of HBM per device.

```python
import jax
import jax.numpy as jnp
from jax import lax

C = 256
HID = 1024
NLON = 270
NLAT = 32
NDRAW = 2


def touch_ends(array, own_key, least, top_value):
    longest = array.shape.index(max(array.shape))
    spots = []
    for shift in (0, 1):
        where = [jax.random.randint(jax.random.fold_in(own_key, axis), (), 0, length) for axis, length in enumerate(array.shape)]
        where[longest] = (where[longest] + shift) % array.shape[longest]
        spots.append(tuple(where))
    return array.at[spots[0]].set(least).at[spots[1]].set(top_value)


def steps_of(key, dims, pieces, least, high):
    def one(axis_at, shards_of):
        heights = jax.random.uniform(jax.random.fold_in(jax.random.fold_in(key, 6), axis_at), (shards_of,), jnp.float32, least / len(pieces), high / len(pieces))
        return jnp.repeat(jnp.exp(heights), dims[axis_at] // shards_of).reshape((-1,) + (1,) * (len(dims) - axis_at - 1))

    gain = one(*pieces[0])
    for cut in pieces[1:]:
        gain = gain * one(*cut)
    return gain


def bell_draw(rng, extent, width, reach, shards=(), held_as=jnp.bfloat16):
    gain = steps_of(rng, extent, shards, -0.22, 0.18) if shards else 1.0
    values = jax.random.normal(rng, extent, jnp.float32) * width * gain
    return jnp.minimum(jnp.maximum(values, -reach), reach).astype(held_as)


def setup_inputs(seed: int = 0, part: int = 0) -> dict:
    splits = jax.random.split(jax.random.key(seed), 13)
    part_keys = jax.random.split(jax.random.fold_in(splits[12], part), 13)
    return {
        "inputs": bell_draw(part_keys[0], (NDRAW, NLAT, NLON, C), 1.0, 6.0, ((0, 2), (1, 8))),
        "land_mask": touch_ends((jax.random.randint(splits[1], (NLAT, NLON), 0, 4) < 3).astype(jnp.int32), jax.random.fold_in(splits[1], 1), 0, 1),
        "kernel": bell_draw(splits[2], (7, 7, C), 49 ** -0.5, 0.875, (), jnp.float32),
        "conv_bias": bell_draw(splits[3], (C,), 0.5, 3.0, (), jnp.float32),
        "norm_gain": jnp.clip(1.0 + 0.18 * jax.random.normal(splits[4], (C,), jnp.float32), 0.1, 1.9),
        "norm_bias": bell_draw(splits[5], (C,), 0.5, 3.0, (), jnp.float32),
        "w_in": bell_draw(splits[6], (C, HID), C ** -0.5, 0.375),
        "b_in": bell_draw(splits[7], (HID,), 0.5, 3.0, (), jnp.float32),
        "w_out": bell_draw(splits[8], (HID, C), HID ** -0.5, 0.1875),
        "b_out": bell_draw(splits[9], (C,), 0.5, 3.0, (), jnp.float32),
        "layer_scale": jnp.clip(1.0 + 0.18 * jax.random.normal(splits[10], (C,), jnp.float32), 0.1, 1.9),
        "cotangent": bell_draw(part_keys[11], (NDRAW, NLAT, NLON, C), 1.0, 6.0, ((0, 2), (1, 8))),
    }


ROOT_TERM = 0.7978845608028654
CUBIC = 0.044715
EPSILON = 1e-06

def lon_wrap(values):
    return jnp.concatenate([values[:, :, -3:], values, values[:, :, :3]], axis=2)

def apply_taps(padded, weights, height, breadth):
    total = jnp.zeros((padded.shape[0], height, breadth, padded.shape[3]), jnp.float32)
    for row_off in range(7):
        for col_off in range(7):
            total = total + padded[:, row_off:row_off + height, col_off:col_off + breadth, :] * weights[row_off, col_off]
    return total

def kernel_terms(padded, grad_map, height, breadth):
    rows_list = []
    for row_off in range(7):
        cells_list = []
        for col_off in range(7):
            window = padded[:, row_off:row_off + height, col_off:col_off + breadth, :]
            cells_list.append(lax.optimization_barrier(jnp.sum(window * grad_map, axis=(0, 1, 2))))
        rows_list.append(jnp.stack(cells_list))
    return jnp.stack(rows_list)

def gelu_slope(hidden):
    inner = ROOT_TERM * (hidden + CUBIC * hidden * hidden * hidden)
    tanh_value = jnp.tanh(inner)
    return 0.5 * (1.0 + tanh_value) + 0.5 * hidden * (1.0 - tanh_value * tanh_value) * ROOT_TERM * (1.0 + 3.0 * CUBIC * hidden * hidden)

def forward_backward(state, padded_state, land_mask, kernel, conv_bias, norm_gain, norm_bias, w_in, b_in, w_out, b_out, layer_scale, cotangent, extend):
    height = state.shape[1]
    breadth = state.shape[2]
    channels = state.shape[3]
    wrapped = lon_wrap(padded_state.astype(jnp.float32))
    conv_out = apply_taps(wrapped, kernel, height, breadth) + conv_bias
    center = lax.optimization_barrier(jnp.mean(conv_out, axis=-1, keepdims=True))
    deviation = conv_out - center
    inv_std = lax.rsqrt(lax.optimization_barrier(jnp.mean(deviation * deviation, axis=-1, keepdims=True)) + EPSILON)
    unit = deviation * inv_std
    normed = (unit * norm_gain + norm_bias).astype(jnp.bfloat16).reshape(-1, channels)
    hidden = jnp.dot(normed, w_in, preferred_element_type=jnp.float32) + b_in
    inner = ROOT_TERM * (hidden + CUBIC * hidden * hidden * hidden)
    activated = (0.5 * hidden * (1.0 + jnp.tanh(inner))).astype(jnp.bfloat16)
    mixed = (jnp.dot(activated, w_out, preferred_element_type=jnp.float32) + b_out).reshape(state.shape)
    ocean = land_mask.astype(jnp.float32)[None, :, :, None]
    output = (state.astype(jnp.float32) + ocean * layer_scale * mixed).astype(jnp.bfloat16)
    upstream = cotangent.astype(jnp.float32)
    scale_part = lax.optimization_barrier(jnp.sum(ocean * upstream * mixed, axis=(0, 1, 2)))
    grad_mixed = (ocean * layer_scale * upstream).astype(jnp.bfloat16).reshape(-1, channels)
    out_bias_part = lax.optimization_barrier(jnp.sum(grad_mixed.astype(jnp.float32), axis=0))
    w_out_part = lax.dot_general(activated, grad_mixed, (((0,), (0,)), ((), ())), preferred_element_type=jnp.float32)
    grad_act = lax.dot_general(grad_mixed, w_out, (((1,), (1,)), ((), ())), preferred_element_type=jnp.float32)
    grad_hidden = (grad_act * gelu_slope(hidden)).astype(jnp.bfloat16)
    w_in_part = lax.dot_general(normed, grad_hidden, (((0,), (0,)), ((), ())), preferred_element_type=jnp.float32)
    hidden_bias_part = lax.optimization_barrier(jnp.sum(grad_hidden.astype(jnp.float32), axis=0))
    grad_normed = lax.dot_general(grad_hidden, w_in, (((1,), (1,)), ((), ())), preferred_element_type=jnp.float32).reshape(state.shape)
    gain_part = lax.optimization_barrier(jnp.sum(grad_normed * unit, axis=(0, 1, 2)))
    nbias_part = lax.optimization_barrier(jnp.sum(grad_normed, axis=(0, 1, 2)))
    scaled = grad_normed * norm_gain
    grad_conv = (inv_std * (scaled - lax.optimization_barrier(jnp.mean(scaled, axis=-1, keepdims=True)) - unit * lax.optimization_barrier(jnp.mean(scaled * unit, axis=-1, keepdims=True)))).astype(jnp.bfloat16)
    grad_float = grad_conv.astype(jnp.float32)
    conv_bias_part = lax.optimization_barrier(jnp.sum(grad_float, axis=(0, 1, 2)))
    kernel_part = kernel_terms(wrapped, grad_float, height, breadth)
    grad_padded = lon_wrap(extend(grad_conv).astype(jnp.float32))
    input_grad = (upstream + apply_taps(grad_padded, kernel[::-1, ::-1], height, breadth)).astype(jnp.bfloat16)
    channel_part = jnp.stack([conv_bias_part, gain_part, nbias_part, out_bias_part, scale_part])
    return (output, input_grad, kernel_part, w_in_part, w_out_part, hidden_bias_part, channel_part)

def lat_zeros(values):
    return jnp.pad(values, ((0, 0), (3, 3), (0, 0), (0, 0)))

def reference(inputs, land_mask, kernel, conv_bias, norm_gain, norm_bias, w_in, b_in, w_out, b_out, layer_scale, cotangent):
    results = forward_backward(inputs, lat_zeros(inputs), land_mask, kernel, conv_bias, norm_gain, norm_bias, w_in, b_in, w_out, b_out, layer_scale, cotangent, lat_zeros)
    output, input_grad, kernel_part, w_in_part, w_out_part, hidden_bias_part, channel_part = results
    factor = 1.0 / jnp.sqrt(jnp.float32(NDRAW * NLAT * NLON))
    return (output, input_grad, kernel_part * factor, w_in_part * factor, w_out_part * factor, hidden_bias_part * factor, channel_part * factor)
```

```python
import functools

import jax
import jax.numpy as jnp
from jax import lax
from jax.experimental import pallas as pl
from jax.experimental.pallas import tpu as pltpu
from jax.sharding import PartitionSpec as P

ROOT_TERM = 0.7978845608028654
CUBIC = 0.044715
EPSILON = 1e-06
F32 = jnp.float32
BF16 = jnp.bfloat16


def block_kernel(
    n,
    scale,
    x_ref,
    cot_ref,
    mask_ref,
    kern_ref,
    conv_bias_ref,
    gain_ref,
    nbias_ref,
    w_in_hbm,
    b_in_ref,
    w_out_hbm,
    b_out_ref,
    ls_ref,
    out_ref,
    igrad_ref,
    wi_ref,
    wo_ref,
    rows_ref,
    xo,
    x_top,
    x_bot,
    cotb,
    mbuf,
    mpad,
    ocean_v,
    taps,
    w_in_ref,
    w_out_ref,
    cot,
    wrap,
    xs,
    acc,
    hid,
    slope_v,
    act,
    gh,
    normed,
    gmix,
    gb,
    g_top,
    g_bot,
    gf,
    rstd_v,
    mixed_v,
    out_v,
    igrad_v,
    bsum,
    chan,
    part,
    r1,
    r2,
    r3,
    whole,
    sm,
    s1,
    s2,
    s3,
    s5,
    s6,
    in_send,
    in_recv,
    in_local,
    back_send,
    back_recv,
    back_local,
    w_local,
    halo_send,
    halo_recv,
    send_sem,
    recv_sem,
    z_send,
    z_recv,
):
    H, W, C = x_ref.shape
    Wp = gb.shape[1]
    B = Wp // 8
    HID = w_in_ref.shape[1]
    m = n // 2
    g = lax.axis_index("group")
    t = lax.axis_index("tile")
    d = lax.axis_index("draw")
    zz = t // 2
    yy = lax.rem(t, 2)
    ty = t + 1 - 2 * yy
    core = (g, t, 1 - d)
    beside = (g, ty, d)
    diag = (g, ty, 1 - d)
    home = yy == d
    away = yy != d
    v = 2 * zz + d

    def at_row(block):
        return (g, 2 * (block // 2) + yy, lax.rem(block, 2))

    up = at_row(lax.rem(v + n - 1, n))
    down = at_row(lax.rem(v + 1, n))
    zpeer = [(g, 2 * lax.rem(zz + k, m) + yy, d) for k in range(m)]

    def remote(src, dst, ss, rs, dev):
        return pltpu.make_async_remote_copy(
            src_ref=src,
            dst_ref=dst,
            send_sem=ss,
            recv_sem=rs,
            device_id=dev,
            device_id_type=pl.DeviceIdType.MESH,
        )

    def moved(src, dst, k):
        return remote(src, dst, in_send.at[k], in_recv.at[k], diag)

    def kept(src, dst, k):
        return pltpu.make_async_copy(src, dst, in_local.at[k])

    load_w = [
        pltpu.make_async_copy(w_in_hbm, w_in_ref, w_local.at[0]),
        pltpu.make_async_copy(w_out_hbm, w_out_ref, w_local.at[1]),
    ]

    @pl.when(home)
    def _():
        for p in range(H):
            kept(x_ref.at[p], xo.at[p], p).start()
        kept(mask_ref, mbuf, 2 * H).start()

    for copy in load_w:
        copy.start()
    barrier = pltpu.get_barrier_semaphore()
    for dev in [core, beside, diag, up, down] + zpeer[1:]:
        pl.semaphore_signal(barrier, inc=1, device_id=dev, device_id_type=pl.DeviceIdType.MESH)
    pl.semaphore_wait(barrier, m + 4)

    def nth(k, end):
        return k + end * (H - 1 - 2 * k)

    @pl.when(away)
    def _():
        for k in range(H):
            p = nth(k, yy)
            moved(x_ref.at[p], xo.at[p], p).start()
        moved(mask_ref, mbuf, 2 * H).start()

    @pl.when(home)
    def _():
        for p in range(H):
            kept(cot_ref.at[p], cotb.at[p], H + p).start()

    for k in range(49):
        taps[k] = jnp.broadcast_to(kern_ref[k // 7, k % 7 : k % 7 + 1, :], (8, C))

    @pl.when(v == 0)
    def _():
        x_top[...] = jnp.zeros_like(x_top)
        g_top[...] = jnp.zeros_like(g_top)

    @pl.when(v == n - 1)
    def _():
        x_bot[...] = jnp.zeros_like(x_bot)
        g_bot[...] = jnp.zeros_like(g_bot)

    def to_up(own, bot, a, at):
        k = at + a
        return remote(own.at[a], bot.at[a], halo_send.at[k], halo_recv.at[k], up)

    def to_down(own, top, a, at):
        k = at + 3 + a
        return remote(own.at[a + H - 3], top.at[a], halo_send.at[k], halo_recv.at[k], down)

    def row_ready(own, top, bot, at, q):
        @pl.when(jnp.logical_and(v > 0, q < 3))
        def _():
            to_up(own, bot, q, at).start()

        @pl.when(jnp.logical_and(v < n - 1, q >= H - 3))
        def _():
            to_down(own, top, q - (H - 3), at).start()

    def halo_arrive(own, top, bot, at, ups, downs):
        @pl.when(v > 0)
        def _():
            for a in downs:
                to_down(own, top, a, at).wait_recv()

        @pl.when(v < n - 1)
        def _():
            for a in ups:
                to_up(own, bot, a, at).wait_recv()

    def halo_sent(own, top, bot, at):
        @pl.when(v > 0)
        def _():
            for a in range(3):
                to_up(own, bot, a, at).wait_send()

        @pl.when(v < n - 1)
        def _():
            for a in range(3):
                to_down(own, top, a, at).wait_send()

    x_side = (xo, x_top, x_bot, 0)
    g_side = (gb, g_top, g_bot, 6)

    def spread(value, dst, row):
        rows = value.shape[0]
        wrap[8 : 8 + rows] = value.astype(F32)
        wrap[5:8] = wrap[5 + W : 8 + W]
        wrap[8 + W : 16 + W] = wrap[8:16]
        for j in range(7):
            dst[j, row] = wrap[5 + j : 5 + j + Wp].reshape(B, 8, C)

    def halo_spread(top, bot, dst, ups, downs):
        for a in downs:
            spread(top[a], dst, a)
        for a in ups:
            spread(bot[a], dst, a + H + 3)

    def conv(src, rows, flip, first, outs=tuple(range(4))):
        @pl.loop(0, B // 2)
        def _(c):
            q = pl.ds(c * 2, 2)
            live = [p for p in outs if any(0 <= r - p < 7 for r in rows)]
            sums = [acc[p, q] if p in live and not first else None for p in range(H)]
            for j in range(7):
                for r in rows:
                    cells = src[j, r, q]
                    for p in live:
                        i = r - p
                        if 0 <= i < 7:
                            tap = (6 - i) * 7 + 6 - j if flip else i * 7 + j
                            term = cells * taps[tap][None]
                            sums[p] = term if sums[p] is None else sums[p] + term
            for p in live:
                acc[p, q] = sums[p]

    own_rows = list(range(3, H + 3))

    @pl.loop(0, H)
    def _(k):
        q = nth(k, d)

        @pl.when(home)
        def _():
            kept(x_ref.at[q], xo.at[q], q).wait()

        @pl.when(away)
        def _():
            moved(x_ref.at[q], xo.at[q], q).wait_recv()

        row_ready(*x_side, q)
        spread(xo[q], xs, q + 3)

    @pl.when(away)
    def _():
        for p in range(H):
            moved(x_ref.at[p], xo.at[p], p).wait_send()
        for p in range(H):
            moved(cot_ref.at[p], cotb.at[p], H + p).start()

    conv(xs, own_rows, False, True)

    @pl.when(home)
    def _():
        kept(mask_ref, mbuf, 2 * H).wait()

    @pl.when(away)
    def _():
        moved(mask_ref, mbuf, 2 * H).wait()

    mpad[...] = jnp.zeros_like(mpad)
    mpad[0:H, 0:W] = mbuf[...].astype(F32)
    flags = mpad[...].astype(BF16)
    lines = lax.broadcasted_iota(jnp.int32, (mpad.shape[0], C), 0)
    for p in range(H):
        pick = jnp.where(lines == p, 1.0, 0.0).astype(BF16)
        ocean_v[p] = lax.dot_general(
            flags, pick, (((0,), (0,)), ((), ())), preferred_element_type=F32
        ).astype(BF16)
    bsum[...] = jnp.zeros_like(bsum)
    chan[...] = jnp.zeros_like(chan)
    for copy in load_w:
        copy.wait()
    halo_arrive(*x_side, [0, 1, 2], [0, 1, 2])
    halo_spread(x_top, x_bot, xs, [0, 1, 2], [0, 1, 2])
    conv(xs, [0, 1, 2, H + 3, H + 4, H + 5], False, False)

    def rowsum(value):
        return jnp.sum(value, axis=0, keepdims=True)

    def give_back(src, dst, k):
        return remote(src, dst, back_send.at[k], back_recv.at[k], diag)

    def put(src, dst, k):
        return pltpu.make_async_copy(src, dst, back_local.at[k])

    def returned(src, dst, k):
        @pl.when(home)
        def _():
            put(src, dst, k).start()

        @pl.when(away)
        def _():
            give_back(src, dst, k).start()

    @pl.loop(0, H)
    def _(p):
        conv_out = acc[p].reshape(Wp, C) + conv_bias_ref[...]
        dev = conv_out - jnp.mean(conv_out, axis=-1, keepdims=True)
        rstd = lax.rsqrt(jnp.mean(dev * dev, axis=-1, keepdims=True) + EPSILON)
        unit = dev * rstd
        rstd_v[p] = jnp.broadcast_to(rstd, (Wp, 128))
        gf[p] = unit
        normed[p] = (unit * gain_ref[...] + nbias_ref[...]).astype(BF16)
        hid[...] = jnp.dot(normed[p], w_in_ref[...], preferred_element_type=F32)

        @pl.loop(0, Wp // 16)
        def _(c):
            q = pl.ds(pl.multiple_of(c * 16, 16), 16)
            h = hid[q] + b_in_ref[...]
            h2 = h * h
            th = jnp.tanh(h * (h2 * (ROOT_TERM * CUBIC) + ROOT_TERM))
            half = 0.5 * th + 0.5
            a = h * half
            act[p, q] = a.astype(BF16)
            slope_v[p, q] = half + (a - a * th) * (h2 * (3.0 * CUBIC * ROOT_TERM) + ROOT_TERM)

        mixed = jnp.dot(act[p], w_out_ref[...], preferred_element_type=F32) + b_out_ref[...]
        mixed_v[p] = mixed
        ocean = ocean_v[p].astype(F32)
        out_v[p] = (xo[p].astype(F32) + (ocean * ls_ref[...] * mixed)[0:W]).astype(BF16)
        returned(out_v.at[p], out_ref.at[p], p)

    @pl.when(home)
    def _():
        for p in range(H):
            kept(cot_ref.at[p], cotb.at[p], H + p).wait()

    @pl.when(away)
    def _():
        for p in range(H):
            moved(cot_ref.at[p], cotb.at[p], H + p).wait()

    @pl.loop(0, H)
    def _(p):
        cot[p, 0:W] = cotb[p].astype(F32)
        cot[p, W:Wp] = jnp.zeros((Wp - W, C), F32)
        masked = ocean_v[p].astype(F32) * cot[p]
        grad_mixed = (ls_ref[...] * masked).astype(BF16)
        gmix[p] = grad_mixed
        chan[3:4] += rowsum(grad_mixed.astype(F32))
        chan[4:5] += rowsum(masked * mixed_v[p])

    flat = H * Wp
    T = part.shape[4]
    tiles = 4 * m * T
    per = C // 16

    class Exchange:
        def __init__(self, w):
            self.w = w
            self.s = 4 * w
            self.z = 2 * (m - 1) * w

        def fill(self, tile):
            for k in range(tiles):
                part[self.w, k // (tiles // 2), k // (tiles // 4) % 2, k // T % m, k % T] = tile(
                    k
                ).astype(BF16)
            self.one().start()

        def one(self):
            w, s = self.w, self.s
            return remote(part.at[w, 1 - d], r1.at[w], send_sem.at[s], recv_sem.at[s], core)

        def two(self):
            w, s = self.w, self.s + 1
            return remote(r1.at[w, 1 - yy], r2.at[w], send_sem.at[s], recv_sem.at[s], beside)

        def three(self):
            w = self.w
            return [
                remote(
                    r2.at[w, lax.rem(zz + k, m)],
                    r3.at[w, k - 1],
                    z_send.at[self.z + k - 1],
                    z_recv.at[self.z + k - 1],
                    zpeer[k],
                )
                for k in range(1, m)
            ]

        def four(self):
            mine = whole.at[self.w, d, yy, zz]
            return [
                remote(
                    mine,
                    mine,
                    z_send.at[self.z + m - 2 + k],
                    z_recv.at[self.z + m - 2 + k],
                    zpeer[k],
                )
                for k in range(1, m)
            ]

        def five(self):
            mine = whole.at[self.w, d, yy]
            s = self.s + 2
            return remote(mine, mine, send_sem.at[s], recv_sem.at[s], beside)

        def six(self):
            mine = whole.at[self.w, d]
            s = self.s + 3
            return remote(mine, mine, send_sem.at[s], recv_sem.at[s], core)

        def after_one(self):
            w = self.w
            self.one().wait()
            r1[w] = (part[w, d].astype(F32) + r1[w].astype(F32)).astype(BF16)
            self.two().start()

        def after_two(self):
            w = self.w
            self.two().wait()
            r2[w] = (r1[w, yy].astype(F32) + r2[w].astype(F32)).astype(BF16)
            for copy in self.three():
                copy.start()

        def after_three(self):
            w = self.w
            for copy in self.three():
                copy.wait()
            total = r2[w, zz].astype(F32)
            for k in range(m - 1):
                total = total + r3[w, k].astype(F32)
            whole[w, d, yy, zz] = (total * scale).astype(BF16)
            for copy in self.four():
                copy.start()

        def after_four(self):
            for copy in self.four():
                copy.wait()
            self.five().start()

        def after_five(self):
            self.five().wait()
            self.six().start()

        def after_six(self):
            self.six().wait()

    ex_out = Exchange(0)
    ex_in = Exchange(1)

    d_out = lax.dot_general(
        gmix[...].reshape(flat, C),
        act[...].reshape(flat, HID),
        (((0,), (0,)), ((), ())),
        preferred_element_type=F32,
    ).T
    ex_out.fill(lambda k: d_out[k * 16 : k * 16 + 16])

    @pl.loop(0, H)
    def _(k):
        p = nth(k, d)
        hid[...] = lax.dot_general(
            gmix[p], w_out_ref[...], (((1,), (1,)), ((), ())), preferred_element_type=F32
        )

        @pl.loop(0, Wp // 16)
        def _(c):
            q = pl.ds(pl.multiple_of(c * 16, 16), 16)
            grad_hidden = (hid[q] * slope_v[p, q]).astype(BF16)
            gh[p, q] = grad_hidden
            wide = grad_hidden.astype(F32)
            bsum[...] += wide[0:8] + wide[8:16]

        grad_normed = lax.dot_general(
            gh[p], w_in_ref[...], (((1,), (1,)), ((), ())), preferred_element_type=F32
        )
        unit = gf[p]
        scaled = grad_normed * gain_ref[...]
        grad_conv = rstd_v[p][:, 0:1] * (
            scaled
            - jnp.mean(scaled, axis=-1, keepdims=True)
            - unit * jnp.mean(scaled * unit, axis=-1, keepdims=True)
        )
        rounded = grad_conv.astype(BF16)
        gb[p] = rounded
        row_ready(*g_side, p)
        chan[0:1] += rowsum(rounded.astype(F32))
        chan[1:2] += rowsum(grad_normed * unit)
        chan[2:3] += rowsum(grad_normed)

        @pl.when(k == 0)
        def _():
            ex_out.after_one()

        @pl.when(k == 2)
        def _():
            ex_out.after_two()

    d_in = lax.dot_general(
        normed[...].reshape(flat, C),
        gh[...].reshape(flat, HID),
        (((0,), (0,)), ((), ())),
        preferred_element_type=F32,
    )
    ex_in.fill(
        lambda k: d_in[k % per * 16 : k % per * 16 + 16, k // per * C : k // per * C + C]
    )
    ex_out.after_three()

    for j in range(7):

        def tap_terms(c, sums):
            q = pl.ds(c * 2, 2)
            cells16 = pl.ds(pl.multiple_of(c * 16, 16), 16)
            grads = [gb[p, cells16].astype(F32).reshape(2, 8, C) for p in range(H)]
            sums = list(sums)
            for r in range(H + 6):
                cells = xs[j, r, q]
                for p in range(H):
                    i = r - p
                    if 0 <= i < 7:
                        term = cells * grads[p]
                        sums[i] = sums[i] + (term[0] + term[1])
            return tuple(sums)

        sums = lax.fori_loop(0, B // 2, tap_terms, tuple(jnp.zeros((8, C), F32) for _ in range(7)))
        for i in range(7):
            k = i * 7 + j
            sm[k // 32, k % 32 : k % 32 + 1] = rowsum(sums[i])
        if j == 1:
            ex_in.after_one()
        if j == 4:
            ex_in.after_two()
            ex_out.after_four()

    hidden_sum = rowsum(bsum[...])
    for k in range(HID // C):
        sm[1, 17 + k : 18 + k] = hidden_sum[:, k * C : k * C + C]
    sm[1, 21:26] = chan[0:5]
    sm[1, 26:32] = jnp.zeros((6, C), F32)

    small1 = remote(sm.at[1 - d], s1, send_sem.at[8], recv_sem.at[8], core)
    small1.start()

    @pl.loop(0, H)
    def _(r):
        spread(gb[r], xs, r + 3)

    ex_in.after_three()
    small1.wait()
    s2[...] = sm[d] + s1[...]
    small2 = remote(s2, s3, send_sem.at[9], recv_sem.at[9], beside)
    small2.start()
    ex_out.after_five()

    halo_arrive(*g_side, [0, 1, 2], [0, 1, 2])
    halo_spread(g_top, g_bot, xs, [0, 1, 2], [0, 1, 2])
    near, far = (0, 1), (2, 3)

    def finish(rows):
        for p in rows:
            igrad_v[p] = (cot[p] + acc[p].reshape(Wp, C)).astype(BF16)[0:W]
            returned(igrad_v.at[p], igrad_ref.at[p], H + p)

    conv(xs, list(range(0, 8)), True, True, near)
    finish(near)
    ex_in.after_four()
    small2.wait()
    s5[zz] = s2[...] + s3[...]
    zs = 4 * (m - 1) - 1
    small3 = [
        remote(s5.at[zz], s5.at[zz], z_send.at[zs + k], z_recv.at[zs + k], zpeer[k])
        for k in range(1, m)
    ]
    for copy in small3:
        copy.start()
    conv(xs, list(range(2, 10)), True, True, far)
    finish(far)
    ex_in.after_five()
    for copy in small3:
        copy.wait()
    small_total = s5[0]
    for k in range(1, m):
        small_total = small_total + s5[k]
    s6[d] = small_total * scale
    small4 = remote(s6.at[d], s6.at[d], send_sem.at[10], recv_sem.at[10], core)
    small4.start()
    halo_sent(*x_side)
    halo_sent(*g_side)
    ex_out.after_six()
    last = [pltpu.make_async_copy(whole.at[0], wo_ref, w_local.at[0])]
    last[0].start()
    small4.wait()
    last.append(pltpu.make_async_copy(s6, rows_ref, w_local.at[2]))
    last[1].start()
    ex_in.after_six()
    last.append(pltpu.make_async_copy(whole.at[1], wi_ref, w_local.at[1]))
    last[2].start()
    for k in range(2 * H):
        src, dst = ((out_v, out_ref), (igrad_v, igrad_ref))[k // H]

        @pl.when(home)
        def _():
            put(src.at[k % H], dst.at[k % H], k).wait()

        @pl.when(away)
        def _():
            give_back(src.at[k % H], dst.at[k % H], k).wait()

    for copy in last:
        copy.wait()


def gather_kernel(wi_part, wo_part, rows_part, wi_ref, wo_ref, kgrad_ref, bgrad_ref, chan_ref):
    C = wi_ref.shape[0]
    HID = wi_ref.shape[1]
    per = C // 16
    _, _, m, T, _, _ = wi_part.shape
    tiles = 4 * m * T
    rows = rows_part[...].reshape(64, C)
    for i in range(7):
        kgrad_ref[i] = rows[i * 7 : i * 7 + 7]
    for k in range(HID // C):
        bgrad_ref[0:1, k * C : k * C + C] = rows[49 + k : 50 + k]
    chan_ref[...] = rows[49 + HID // C : 54 + HID // C]
    for k in range(tiles):
        at = (k // (tiles // 2), k // (tiles // 4) % 2, k // T % m, k % T)
        rb, cb = k % per, k // per
        wi_ref[rb * 16 : rb * 16 + 16, cb * C : cb * C + C] = wi_part[at].astype(F32)
        wo_ref[k * 16 : k * 16 + 16] = wo_part[at].astype(F32)


def per_device(
    n,
    draws,
    inputs,
    land_mask,
    kernel,
    conv_bias,
    norm_gain,
    norm_bias,
    w_in,
    b_in,
    w_out,
    b_out,
    layer_scale,
    cotangent,
):
    _, H, W, C = inputs.shape
    HID = w_in.shape[1]
    Wp = (W + 15) // 16 * 16
    B = Wp // 8
    m = n // 2
    T = HID // 16 // (2 * n)
    scale = float(1.0 / (draws * H * n * W) ** 0.5)
    vm = pl.BlockSpec(memory_space=pltpu.VMEM)
    hbm = pl.BlockSpec(memory_space=pl.ANY)
    scratch = [
        ((H, W, C), BF16),
        ((3, W, C), BF16),
        ((3, W, C), BF16),
        ((H, W, C), BF16),
        ((H, W), jnp.int32),
        ((16, Wp), F32),
        ((H, Wp, C), BF16),
        ((49, 8, C), F32),
        ((C, HID), BF16),
        ((HID, C), BF16),
        ((H, Wp, C), F32),
        ((Wp + 16, C), F32),
        ((7, H + 6, B, 8, C), F32),
        ((H, B, 8, C), F32),
        ((Wp, HID), F32),
        ((H, Wp, HID), F32),
        ((H, Wp, HID), BF16),
        ((H, Wp, HID), BF16),
        ((H, Wp, C), BF16),
        ((H, Wp, C), BF16),
        ((H, Wp, C), BF16),
        ((3, Wp, C), BF16),
        ((3, Wp, C), BF16),
        ((H, Wp, C), F32),
        ((H, Wp, 128), F32),
        ((H, Wp, C), F32),
        ((H, W, C), BF16),
        ((H, W, C), BF16),
        ((8, HID), F32),
        ((8, C), F32),
        ((2, 2, 2, m, T, 16, C), BF16),
        ((2, 2, m, T, 16, C), BF16),
        ((2, m, T, 16, C), BF16),
        ((2, m - 1, T, 16, C), BF16),
        ((2, 2, 2, m, T, 16, C), BF16),
        ((2, 32, C), F32),
        ((32, C), F32),
        ((32, C), F32),
        ((32, C), F32),
        ((m, 32, C), F32),
        ((2, 32, C), F32),
    ]
    dma = pltpu.SemaphoreType.DMA
    output, input_grad, wi_part, wo_part, rows_part = pl.pallas_call(
        functools.partial(block_kernel, n, scale),
        out_shape=(
            jax.ShapeDtypeStruct((H, W, C), BF16),
            jax.ShapeDtypeStruct((H, W, C), BF16),
            jax.ShapeDtypeStruct((2, 2, m, T, 16, C), BF16),
            jax.ShapeDtypeStruct((2, 2, m, T, 16, C), BF16),
            jax.ShapeDtypeStruct((2, 32, C), F32),
        ),
        in_specs=[hbm, hbm, hbm, vm, vm, vm, vm, hbm, vm, hbm, vm, vm],
        out_specs=[hbm] * 5,
        scratch_shapes=[pltpu.VMEM(shape, dtype) for shape, dtype in scratch]
        + [
            dma((2 * H + 1,)),
            dma((2 * H + 1,)),
            dma((2 * H + 1,)),
            dma((2 * H,)),
            dma((2 * H,)),
            dma((2 * H,)),
            dma((3,)),
            dma((12,)),
            dma((12,)),
            dma((11,)),
            dma((11,)),
            dma((5 * (m - 1),)),
            dma((5 * (m - 1),)),
        ],
        compiler_params=pltpu.CompilerParams(
            collective_id=0, has_side_effects=True, vmem_limit_bytes=60 * 1024 * 1024
        ),
        name="block",
    )(
        inputs[0],
        cotangent[0],
        land_mask,
        kernel,
        conv_bias[None],
        norm_gain[None],
        norm_bias[None],
        w_in,
        b_in[None],
        w_out,
        b_out[None],
        layer_scale[None],
    )
    w_in_grad, w_out_grad, kernel_grad, b_in_grad, channel = pl.pallas_call(
        gather_kernel,
        out_shape=(
            jax.ShapeDtypeStruct((C, HID), F32),
            jax.ShapeDtypeStruct((HID, C), F32),
            jax.ShapeDtypeStruct((7, 7, C), F32),
            jax.ShapeDtypeStruct((1, HID), F32),
            jax.ShapeDtypeStruct((5, C), F32),
        ),
        in_specs=[vm] * 3,
        out_specs=[vm] * 5,
        name="gather",
    )(wi_part, wo_part, rows_part)
    return (
        output[None],
        input_grad[None],
        kernel_grad,
        w_in_grad,
        w_out_grad,
        b_in_grad[0],
        channel,
    )


def solution(mesh):
    field = P(("group", "draw"), "tile", None, None)
    placed = (field, P("tile", None)) + (P(),) * 9 + (field,)
    return jax.shard_map(
        functools.partial(per_device, mesh.shape["tile"], mesh.shape["draw"]),
        mesh=mesh,
        in_specs=placed,
        out_specs=(
            field,
            field,
            P("group", None, None),
            P("group", None),
            P("group", None),
            P("group"),
            P("group", None),
        ),
        check_vma=False,
    )
```

```python
import functools

import jax
import jax.numpy as jnp
from jax import lax
from jax.experimental import pallas as pl
from jax.experimental.pallas import tpu as pltpu
from jax.sharding import PartitionSpec as P

ROOT_TERM = 0.7978845608028654
CUBIC = 0.044715
EPSILON = 1e-06
F32 = jnp.float32
BF16 = jnp.bfloat16


def block_kernel(
    n,
    scale,
    x_ref,
    cot_ref,
    mask_ref,
    kern_ref,
    conv_bias_ref,
    gain_ref,
    nbias_ref,
    w_in_hbm,
    b_in_ref,
    w_out_hbm,
    b_out_ref,
    ls_ref,
    out_ref,
    igrad_ref,
    wi_ref,
    wo_ref,
    rows_ref,
    xo,
    x_top,
    x_bot,
    cotb,
    mbuf,
    mpad,
    ocean_v,
    taps,
    w_in_ref,
    w_out_ref,
    wx,
    xs,
    acc,
    hid,
    slope_v,
    act,
    gh,
    normed,
    gmix,
    gb,
    g_top,
    g_bot,
    gf,
    rstd_v,
    mixed_v,
    out_v,
    igrad_v,
    bsum,
    chan,
    part,
    r1,
    r2,
    r3,
    whole,
    sm,
    s1,
    s2,
    s3,
    s5,
    s6,
    in_send,
    in_recv,
    in_local,
    back_send,
    back_recv,
    back_local,
    w_local,
    halo_send,
    halo_recv,
    send_sem,
    recv_sem,
    z_send,
    z_recv,
):
    H, Wp, C = x_ref.shape
    W = mbuf.shape[1]
    B = Wp // 8
    HID = w_in_ref.shape[1]
    U = Wp // 16
    ends = [(U * k + 3) // 4 * 16 for k in range(5)]
    chunks = list(zip(ends[:-1], ends[1:]))
    inner = [0] + [e + 16 for e in ends[1:-1]] + [Wp - 16]
    segs = [(Wp - 16, Wp)] + list(zip(inner[:-1], inner[1:]))
    m = n // 2
    g = lax.axis_index("group")
    t = lax.axis_index("tile")
    d = lax.axis_index("draw")
    zz = t // 2
    yy = lax.rem(t, 2)
    ty = t + 1 - 2 * yy
    core = (g, t, 1 - d)
    beside = (g, ty, d)
    diag = (g, ty, 1 - d)
    home = yy == d
    away = yy != d
    v = 2 * zz + d

    def at_row(block):
        return (g, 2 * (block // 2) + yy, lax.rem(block, 2))

    up = at_row(lax.rem(v + n - 1, n))
    down = at_row(lax.rem(v + 1, n))
    zpeer = [(g, 2 * lax.rem(zz + k, m) + yy, d) for k in range(m)]

    def remote(src, dst, ss, rs, dev):
        return pltpu.make_async_remote_copy(
            src_ref=src,
            dst_ref=dst,
            send_sem=ss,
            recv_sem=rs,
            device_id=dev,
            device_id_type=pl.DeviceIdType.MESH,
        )

    def moved(src, dst, k):
        return remote(src, dst, in_send.at[k], in_recv.at[k], diag)

    def kept(src, dst, k):
        return pltpu.make_async_copy(src, dst, in_local.at[k])

    load_w = [
        pltpu.make_async_copy(w_in_hbm, w_in_ref, w_local.at[0]),
        pltpu.make_async_copy(w_out_hbm, w_out_ref, w_local.at[1]),
    ]

    def seg(ref, k):
        lo, hi = segs[k]
        return ref.at[:, lo:hi]

    def chunk(ref, k):
        lo, hi = chunks[k]
        return ref.at[:, lo:hi]

    N = len(segs)
    K = len(chunks)

    def x_args(k):
        return seg(x_ref, k), seg(xo, k), k

    def cot_args(k):
        return chunk(cot_ref, k), chunk(cotb, k), N + k

    mask_args = (mask_ref, mbuf, N + K)

    @pl.when(home)
    def _():
        for k in range(N):
            kept(*x_args(k)).start()
        kept(*mask_args).start()

    for copy in load_w:
        copy.start()
    barrier = pltpu.get_barrier_semaphore()
    for dev in [core, beside, diag, up, down] + zpeer[1:]:
        pl.semaphore_signal(barrier, inc=1, device_id=dev, device_id_type=pl.DeviceIdType.MESH)
    pl.semaphore_wait(barrier, m + 4)

    @pl.when(away)
    def _():
        for k in range(N):
            moved(*x_args(k)).start()
        moved(*mask_args).start()

    @pl.when(home)
    def _():
        for k in range(K):
            kept(*cot_args(k)).start()

    for k in range(49):
        taps[k] = jnp.broadcast_to(kern_ref[k // 7, k % 7 : k % 7 + 1, :], (8, C))

    @pl.when(v == 0)
    def _():
        x_top[...] = jnp.zeros_like(x_top)
        g_top[...] = jnp.zeros_like(g_top)

    @pl.when(v == n - 1)
    def _():
        x_bot[...] = jnp.zeros_like(x_bot)
        g_bot[...] = jnp.zeros_like(g_bot)

    def to_up(own, bot, span, k):
        lo, hi = span
        return remote(
            own.at[0:3, lo:hi], bot.at[:, lo:hi], halo_send.at[2 * k], halo_recv.at[2 * k], up
        )

    def to_down(own, top, span, k):
        lo, hi = span
        k = 2 * k + 1
        return remote(
            own.at[H - 3 : H, lo:hi], top.at[:, lo:hi], halo_send.at[k], halo_recv.at[k], down
        )

    def halo_start(own, top, bot, span, k):
        @pl.when(v > 0)
        def _():
            to_up(own, bot, span, k).start()

        @pl.when(v < n - 1)
        def _():
            to_down(own, top, span, k).start()

    def halo_arrive(own, top, bot, span, k):
        @pl.when(v > 0)
        def _():
            to_down(own, top, span, k).wait_recv()

        @pl.when(v < n - 1)
        def _():
            to_up(own, bot, span, k).wait_recv()

    def halo_sent(own, top, bot, span, k):
        @pl.when(v > 0)
        def _():
            to_up(own, bot, span, k).wait_send()

        @pl.when(v < n - 1)
        def _():
            to_down(own, top, span, k).wait_send()

    x_side = (xo, x_top, x_bot)
    g_side = (gb, g_top, g_bot)

    def widen(value, first, lo):
        rows, size, _ = value.shape
        wx[first : first + rows, 8 + lo : 8 + lo + size] = value.astype(F32)

    def spread(span):
        lo, hi = span

        @pl.loop(0, H + 6)
        def _(r):
            for j in range(7):
                xs[j, r, lo // 8 : hi // 8] = wx[r, 5 + j + lo : 5 + j + hi].reshape(
                    (hi - lo) // 8, 8, C
                )

    def wrap_left():
        wx[:, 5:8] = wx[:, 5 + W : 8 + W]

    def wrap_right():
        wx[:, 8 + W : 16 + W] = wx[:, 8:16]

    def conv(span, flip):
        for j in range(7):
            column = [taps[(6 - i) * 7 + 6 - j if flip else i * 7 + j][None] for i in range(7)]

            @pl.loop(span[0] // 16, span[1] // 16)
            def _(c):
                q = pl.ds(c * 2, 2)
                sums = [acc[p, q] if j else None for p in range(H)]
                for r in range(H + 6):
                    cells = xs[j, r, q]
                    for p in range(H):
                        i = r - p
                        if 0 <= i < 7:
                            term = cells * column[i]
                            sums[p] = term if sums[p] is None else sums[p] + term
                for p in range(H):
                    acc[p, q] = sums[p]

    def x_seg(k):
        @pl.when(home)
        def _():
            kept(*x_args(k)).wait()

        @pl.when(away)
        def _():
            moved(*x_args(k)).wait_recv()

        halo_start(*x_side, segs[k], k)
        lo, hi = segs[k]
        widen(xo[:, lo:hi], 3, lo)

    def x_halo(k):
        halo_arrive(*x_side, segs[k], k)
        lo, hi = segs[k]
        widen(x_top[:, lo:hi], 0, lo)
        widen(x_bot[:, lo:hi], H + 3, lo)

    def masks():
        @pl.when(home)
        def _():
            kept(*mask_args).wait()

        @pl.when(away)
        def _():
            moved(*mask_args).wait()

        mpad[...] = jnp.zeros_like(mpad)
        mpad[0:H, 0:W] = mbuf[...].astype(F32)
        flags = mpad[...].astype(BF16)
        lines = lax.broadcasted_iota(jnp.int32, (mpad.shape[0], C), 0)
        for p in range(H):
            pick = jnp.where(lines == p, 1.0, 0.0).astype(BF16)
            ocean_v[p] = lax.dot_general(
                flags, pick, (((0,), (0,)), ((), ())), preferred_element_type=F32
            ).astype(BF16)

    def rowsum(value):
        return jnp.sum(value, axis=0, keepdims=True)

    def give_back(src, dst, k):
        return remote(src, dst, back_send.at[k], back_recv.at[k], diag)

    def put(src, dst, k):
        return pltpu.make_async_copy(src, dst, back_local.at[k])

    def returned(src, dst, k):
        @pl.when(home)
        def _():
            put(src, dst, k).start()

        @pl.when(away)
        def _():
            give_back(src, dst, k).start()

    def cells(k):
        lo, hi = chunks[k]
        return slice(H * lo, H * hi)

    def ocean_of(k):
        lo, hi = chunks[k]
        return ocean_v[:, lo:hi].astype(F32).reshape(H * (hi - lo), C)

    def forward(k):
        lo, hi = chunks[k]
        size = H * (hi - lo)
        at = cells(k)
        conv_out = acc[:, lo // 8 : hi // 8].reshape(size, C) + conv_bias_ref[...]
        dev = conv_out - jnp.mean(conv_out, axis=-1, keepdims=True)
        rstd = lax.rsqrt(jnp.mean(dev * dev, axis=-1, keepdims=True) + EPSILON)
        unit = dev * rstd
        rstd_v[at] = jnp.broadcast_to(rstd, (size, 128))
        gf[at] = unit
        normed[at] = (unit * gain_ref[...] + nbias_ref[...]).astype(BF16)
        hid[0:size] = jnp.dot(normed[at], w_in_ref[...], preferred_element_type=F32)

        @pl.loop(0, size // 16)
        def _(c):
            q = pl.ds(pl.multiple_of(c * 16, 16), 16)
            to = pl.ds(pl.multiple_of(H * lo + c * 16, 16), 16)
            h = hid[q] + b_in_ref[...]
            h2 = h * h
            th = jnp.tanh(h * (h2 * (ROOT_TERM * CUBIC) + ROOT_TERM))
            half = 0.5 * th + 0.5
            a = h * half
            act[to] = a.astype(BF16)
            slope_v[to] = half + (a - a * th) * (h2 * (3.0 * CUBIC * ROOT_TERM) + ROOT_TERM)

        mixed = jnp.dot(act[at], w_out_ref[...], preferred_element_type=F32) + b_out_ref[...]
        mixed_v[at] = mixed
        change = (ocean_of(k) * ls_ref[...] * mixed).reshape(H, hi - lo, C)
        out_v[:, lo:hi] = (xo[:, lo:hi].astype(F32) + change).astype(BF16)
        returned(chunk(out_v, k), chunk(out_ref, k), k)

    for k in range(3):
        x_seg(k)
    masks()
    bsum[...] = jnp.zeros_like(bsum)
    chan[...] = jnp.zeros_like(chan)
    for copy in load_w:
        copy.wait()
    x_halo(0)
    wrap_left()
    for k in range(K):
        x_halo(k + 1)
        if k == 0:
            wrap_right()
        spread(chunks[k])
        conv(chunks[k], False)
        forward(k)
        if k == 0:

            @pl.when(away)
            def _():
                for q in range(N):
                    moved(*x_args(q)).wait_send()
                for q in range(K):
                    moved(*cot_args(q)).start()

            for q in range(3, N):
                x_seg(q)

    for k in range(K):

        @pl.when(home)
        def _():
            kept(*cot_args(k)).wait()

        @pl.when(away)
        def _():
            moved(*cot_args(k)).wait()

        lo, hi = chunks[k]
        size = H * (hi - lo)
        value = cotb[:, lo:hi].astype(F32).reshape(size, C)
        masked = ocean_of(k) * value
        grad_mixed = (ls_ref[...] * masked).astype(BF16)
        gmix[cells(k)] = grad_mixed
        chan[3:4] += rowsum(grad_mixed.astype(F32))
        chan[4:5] += rowsum(masked * mixed_v[cells(k)])

    T = part.shape[4]
    L = part.shape[6]
    tiles = 4 * m * T
    per = C // 16

    class Exchange:
        def __init__(self, w):
            self.w = w
            self.s = 4 * w
            self.z = 2 * (m - 1) * w

        def fill(self, tile):
            for k in range(tiles):
                part[self.w, k // (tiles // 2), k // (tiles // 4) % 2, k // T % m, k % T] = tile(
                    k
                ).astype(BF16)
            self.one().start()

        def one(self):
            w, s = self.w, self.s
            return remote(part.at[w, 1 - d], r1.at[w], send_sem.at[s], recv_sem.at[s], core)

        def two(self):
            w, s = self.w, self.s + 1
            return remote(r1.at[w, 1 - yy], r2.at[w], send_sem.at[s], recv_sem.at[s], beside)

        def three(self):
            w = self.w
            return [
                remote(
                    r2.at[w, lax.rem(zz + k, m)],
                    r3.at[w, k - 1],
                    z_send.at[self.z + k - 1],
                    z_recv.at[self.z + k - 1],
                    zpeer[k],
                )
                for k in range(1, m)
            ]

        def four(self):
            mine = whole.at[self.w, d, yy, zz]
            return [
                remote(
                    mine,
                    mine,
                    z_send.at[self.z + m - 2 + k],
                    z_recv.at[self.z + m - 2 + k],
                    zpeer[k],
                )
                for k in range(1, m)
            ]

        def five(self):
            mine = whole.at[self.w, d, yy]
            s = self.s + 2
            return remote(mine, mine, send_sem.at[s], recv_sem.at[s], beside)

        def six(self):
            mine = whole.at[self.w, d]
            s = self.s + 3
            return remote(mine, mine, send_sem.at[s], recv_sem.at[s], core)

        def after_one(self):
            w = self.w
            self.one().wait()
            r1[w] = (part[w, d].astype(F32) + r1[w].astype(F32)).astype(BF16)
            self.two().start()

        def after_two(self):
            w = self.w
            self.two().wait()
            r2[w] = (r1[w, yy].astype(F32) + r2[w].astype(F32)).astype(BF16)
            for copy in self.three():
                copy.start()

        def after_three(self):
            w = self.w
            for copy in self.three():
                copy.wait()
            total = r2[w, zz].astype(F32)
            for k in range(m - 1):
                total = total + r3[w, k].astype(F32)
            whole[w, d, yy, zz] = (total * scale).astype(BF16)
            for copy in self.four():
                copy.start()

        def after_four(self):
            for copy in self.four():
                copy.wait()
            self.five().start()

        def after_five(self):
            self.five().wait()
            self.six().start()

        def after_six(self):
            self.six().wait()

    ex_out = [Exchange(0), Exchange(1)]
    ex_in = [Exchange(2), Exchange(3)]

    d_out = lax.dot_general(
        gmix[...], act[...], (((0,), (0,)), ((), ())), preferred_element_type=F32
    ).T
    for e in range(2):
        ex_out[e].fill(lambda k: d_out[k * 16 : k * 16 + 16, e * L : e * L + L])

    def grads_hidden(k):
        lo, hi = chunks[k]
        size = H * (hi - lo)
        hid[0:size] = lax.dot_general(
            gmix[cells(k)], w_out_ref[...], (((1,), (1,)), ((), ())), preferred_element_type=F32
        )

        @pl.loop(0, size // 16)
        def _(c):
            q = pl.ds(pl.multiple_of(c * 16, 16), 16)
            to = pl.ds(pl.multiple_of(H * lo + c * 16, 16), 16)
            grad_hidden = (hid[q] * slope_v[to]).astype(BF16)
            gh[to] = grad_hidden
            wide = grad_hidden.astype(F32)
            bsum[...] += wide[0:8] + wide[8:16]

    def grads_conv(k):
        lo, hi = chunks[k]
        at = cells(k)
        grad_normed = lax.dot_general(
            gh[at], w_in_ref[...], (((1,), (1,)), ((), ())), preferred_element_type=F32
        )
        unit = gf[at]
        scaled = grad_normed * gain_ref[...]
        grad_conv = rstd_v[at][:, 0:1] * (
            scaled
            - jnp.mean(scaled, axis=-1, keepdims=True)
            - unit * jnp.mean(scaled * unit, axis=-1, keepdims=True)
        )
        rounded = grad_conv.astype(BF16).reshape(H, hi - lo, C)
        gb[:, lo:hi] = rounded
        halo_start(*g_side, chunks[k], N + k)
        wide = rounded.astype(F32)
        widen(wide, 3, lo)
        chan[0:1] += rowsum(wide.reshape(H * (hi - lo), C))
        chan[1:2] += rowsum(grad_normed * unit)
        chan[2:3] += rowsum(grad_normed)

    for k in range(K):
        grads_hidden(k)
        if k == 1:
            for ex in ex_out:
                ex.after_one()

    d_in = lax.dot_general(
        normed[...], gh[...], (((0,), (0,)), ((), ())), preferred_element_type=F32
    )

    def in_tile(e, k):
        rb, cb = k % per, k // per * C + e * L
        return d_in[rb * 16 : rb * 16 + 16, cb : cb + L]

    for e in range(2):
        ex_in[e].fill(lambda k: in_tile(e, k))
    for ex in ex_out:
        ex.after_two()

    for k in range(K):
        grads_conv(k)
        if k == 1:
            for ex in ex_in:
                ex.after_one()
    ex_in[0].after_two()
    for ex in ex_out:
        ex.after_three()

    for j in range(7):

        def tap_terms(c, sums):
            q = pl.ds(c * 2, 2)
            cells16 = pl.ds(pl.multiple_of(c * 16, 16), 16)
            grads = [gb[p, cells16].astype(F32).reshape(2, 8, C) for p in range(H)]
            sums = list(sums)
            for r in range(H + 6):
                cells = xs[j, r, q]
                for p in range(H):
                    i = r - p
                    if 0 <= i < 7:
                        term = cells * grads[p]
                        sums[i] = sums[i] + (term[0] + term[1])
            return tuple(sums)

        sums = lax.fori_loop(0, B // 2, tap_terms, tuple(jnp.zeros((8, C), F32) for _ in range(7)))
        for i in range(7):
            k = i * 7 + j
            sm[k // 32, k % 32 : k % 32 + 1] = rowsum(sums[i])
        if j == 1:
            ex_in[1].after_two()
        if j == 3:
            ex_in[0].after_three()
            for ex in ex_out:
                ex.after_four()
        if j == 4:
            ex_in[1].after_three()

    hidden_sum = rowsum(bsum[...])
    for k in range(HID // C):
        sm[1, 17 + k : 18 + k] = hidden_sum[:, k * C : k * C + C]
    sm[1, 21:26] = chan[0:5]
    sm[1, 26:32] = jnp.zeros((6, C), F32)

    small1 = remote(sm.at[1 - d], s1, send_sem.at[16], recv_sem.at[16], core)
    small1.start()

    for k in range(K):
        lo, hi = chunks[k]
        halo_arrive(*g_side, chunks[k], N + k)
        widen(g_top[:, lo:hi], 0, lo)
        widen(g_bot[:, lo:hi], H + 3, lo)
    wrap_left()
    wrap_right()
    small1.wait()
    s2[...] = sm[d] + s1[...]
    small2 = remote(s2, s3, send_sem.at[17], recv_sem.at[17], beside)
    small2.start()
    ex_in[0].after_four()
    for ex in ex_out:
        ex.after_five()

    zs = 8 * (m - 1) - 1

    def small3():
        return [
            remote(s5.at[zz], s5.at[zz], z_send.at[zs + k], z_recv.at[zs + k], zpeer[k])
            for k in range(1, m)
        ]

    for k in range(K):
        lo, hi = chunks[k]
        spread(chunks[k])
        conv(chunks[k], True)
        igrad_v[:, lo:hi] = (
            cotb[:, lo:hi].astype(F32) + acc[:, lo // 8 : hi // 8].reshape(H, hi - lo, C)
        ).astype(BF16)
        returned(chunk(igrad_v, k), chunk(igrad_ref, k), K + k)
        if k == 0:
            ex_in[1].after_four()
        if k == 2:
            for ex in ex_in:
                ex.after_five()
        if k == 1:
            small2.wait()
            s5[zz] = s2[...] + s3[...]
            for copy in small3():
                copy.start()

    for copy in small3():
        copy.wait()
    small_total = s5[0]
    for k in range(1, m):
        small_total = small_total + s5[k]
    s6[d] = small_total * scale
    small4 = remote(s6.at[d], s6.at[d], send_sem.at[18], recv_sem.at[18], core)
    small4.start()
    for k in range(N):
        halo_sent(*x_side, segs[k], k)
    for k in range(K):
        halo_sent(*g_side, chunks[k], N + k)
    for ex in ex_out:
        ex.after_six()
    last = [pltpu.make_async_copy(whole.at[0:2], wo_ref, w_local.at[0])]
    last[0].start()
    for ex in ex_in:
        ex.after_six()
    last.append(pltpu.make_async_copy(whole.at[2:4], wi_ref, w_local.at[1]))
    last[1].start()
    small4.wait()
    last.append(pltpu.make_async_copy(s6, rows_ref, w_local.at[2]))
    last[2].start()
    for k in range(2 * K):
        src, dst = ((out_v, out_ref), (igrad_v, igrad_ref))[k // K]
        pair = (chunk(src, k % K), chunk(dst, k % K), k)

        @pl.when(home)
        def _():
            put(*pair).wait()

        @pl.when(away)
        def _():
            give_back(*pair).wait()

    for copy in last:
        copy.wait()


def gather_kernel(wi_part, wo_part, rows_part, wi_ref, wo_ref, kgrad_ref, bgrad_ref, chan_ref):
    C = wi_ref.shape[0]
    HID = wi_ref.shape[1]
    per = C // 16
    _, _, _, m, T, _, L = wi_part.shape
    tiles = 4 * m * T
    rows = rows_part[...].reshape(64, C)
    for i in range(7):
        kgrad_ref[i] = rows[i * 7 : i * 7 + 7]
    for k in range(HID // C):
        bgrad_ref[0:1, k * C : k * C + C] = rows[49 + k : 50 + k]
    chan_ref[...] = rows[49 + HID // C : 54 + HID // C]
    for k in range(tiles):
        at = (k // (tiles // 2), k // (tiles // 4) % 2, k // T % m, k % T)
        rb, cb = k % per, k // per
        for e in range(2):
            wi_ref[rb * 16 : rb * 16 + 16, cb * C + e * L : cb * C + e * L + L] = wi_part[
                (e,) + at
            ].astype(F32)
            wo_ref[k * 16 : k * 16 + 16, e * L : e * L + L] = wo_part[(e,) + at].astype(F32)


def per_device(
    n,
    draws,
    inputs,
    land_mask,
    kernel,
    conv_bias,
    norm_gain,
    norm_bias,
    w_in,
    b_in,
    w_out,
    b_out,
    layer_scale,
    cotangent,
):
    _, H, W, C = inputs.shape
    HID = w_in.shape[1]
    Wp = (W + 15) // 16 * 16
    B = Wp // 8
    m = n // 2
    T = HID // 16 // (2 * n)
    scale = float(1.0 / (draws * H * n * W) ** 0.5)
    vm = pl.BlockSpec(memory_space=pltpu.VMEM)
    hbm = pl.BlockSpec(memory_space=pl.ANY)
    flat = H * Wp
    L = C // 2
    scratch = [
        ((H, Wp, C), BF16),
        ((3, Wp, C), BF16),
        ((3, Wp, C), BF16),
        ((H, Wp, C), BF16),
        ((H, W), jnp.int32),
        ((16, Wp), F32),
        ((H, Wp, C), BF16),
        ((49, 8, C), F32),
        ((C, HID), BF16),
        ((HID, C), BF16),
        ((H + 6, Wp + 16, C), F32),
        ((7, H + 6, B, 8, C), F32),
        ((H, B, 8, C), F32),
        ((flat // 4 + 256, HID), F32),
        ((flat, HID), F32),
        ((flat, HID), BF16),
        ((flat, HID), BF16),
        ((flat, C), BF16),
        ((flat, C), BF16),
        ((H, Wp, C), BF16),
        ((3, Wp, C), BF16),
        ((3, Wp, C), BF16),
        ((flat, C), F32),
        ((flat, 128), F32),
        ((flat, C), F32),
        ((H, Wp, C), BF16),
        ((H, Wp, C), BF16),
        ((8, HID), F32),
        ((8, C), F32),
        ((4, 2, 2, m, T, 16, L), BF16),
        ((4, 2, m, T, 16, L), BF16),
        ((4, m, T, 16, L), BF16),
        ((4, m - 1, T, 16, L), BF16),
        ((4, 2, 2, m, T, 16, L), BF16),
        ((2, 32, C), F32),
        ((32, C), F32),
        ((32, C), F32),
        ((32, C), F32),
        ((m, 32, C), F32),
        ((2, 32, C), F32),
    ]
    dma = pltpu.SemaphoreType.DMA
    output, input_grad, wi_part, wo_part, rows_part = pl.pallas_call(
        functools.partial(block_kernel, n, scale),
        out_shape=(
            jax.ShapeDtypeStruct((H, Wp, C), BF16),
            jax.ShapeDtypeStruct((H, Wp, C), BF16),
            jax.ShapeDtypeStruct((2, 2, 2, m, T, 16, L), BF16),
            jax.ShapeDtypeStruct((2, 2, 2, m, T, 16, L), BF16),
            jax.ShapeDtypeStruct((2, 32, C), F32),
        ),
        in_specs=[hbm, hbm, hbm, vm, vm, vm, vm, hbm, vm, hbm, vm, vm],
        out_specs=[hbm] * 5,
        scratch_shapes=[pltpu.VMEM(shape, dtype) for shape, dtype in scratch]
        + [
            dma((10,)),
            dma((10,)),
            dma((10,)),
            dma((8,)),
            dma((8,)),
            dma((8,)),
            dma((3,)),
            dma((18,)),
            dma((18,)),
            dma((19,)),
            dma((19,)),
            dma((9 * (m - 1),)),
            dma((9 * (m - 1),)),
        ],
        compiler_params=pltpu.CompilerParams(
            collective_id=0, has_side_effects=True, vmem_limit_bytes=60 * 1024 * 1024
        ),
        name="block",
    )(
        jnp.pad(inputs[0], ((0, 0), (0, Wp - W), (0, 0))),
        jnp.pad(cotangent[0], ((0, 0), (0, Wp - W), (0, 0))),
        land_mask,
        kernel,
        conv_bias[None],
        norm_gain[None],
        norm_bias[None],
        w_in,
        b_in[None],
        w_out,
        b_out[None],
        layer_scale[None],
    )
    w_in_grad, w_out_grad, kernel_grad, b_in_grad, channel = pl.pallas_call(
        gather_kernel,
        out_shape=(
            jax.ShapeDtypeStruct((C, HID), F32),
            jax.ShapeDtypeStruct((HID, C), F32),
            jax.ShapeDtypeStruct((7, 7, C), F32),
            jax.ShapeDtypeStruct((1, HID), F32),
            jax.ShapeDtypeStruct((5, C), F32),
        ),
        in_specs=[vm] * 3,
        out_specs=[vm] * 5,
        name="gather",
    )(wi_part, wo_part, rows_part)
    return (
        output[None, :, 0:W],
        input_grad[None, :, 0:W],
        kernel_grad,
        w_in_grad,
        w_out_grad,
        b_in_grad[0],
        channel,
    )


def solution(mesh):
    field = P(("group", "draw"), "tile", None, None)
    placed = (field, P("tile", None)) + (P(),) * 9 + (field,)
    return jax.shard_map(
        functools.partial(per_device, mesh.shape["tile"], mesh.shape["draw"]),
        mesh=mesh,
        in_specs=placed,
        out_specs=(
            field,
            field,
            P("group", None, None),
            P("group", None),
            P("group", None),
            P("group"),
            P("group", None),
        ),
        check_vma=False,
    )
```

```python
import functools

import jax
import jax.numpy as jnp
from jax import lax
from jax.experimental import pallas as pl
from jax.experimental.pallas import tpu as pltpu
from jax.sharding import PartitionSpec as P

ROOT_TERM = 0.7978845608028654
CUBIC = 0.044715
EPSILON = 1e-06
F32 = jnp.float32
BF16 = jnp.bfloat16


def block_kernel(
    n,
    scale,
    x_ref,
    cot_ref,
    mask_ref,
    kern_ref,
    conv_bias_ref,
    gain_ref,
    nbias_ref,
    w_in_hbm,
    b_in_ref,
    w_out_hbm,
    b_out_ref,
    ls_ref,
    out_ref,
    igrad_ref,
    wi_ref,
    wo_ref,
    rows_ref,
    xo,
    x_top,
    x_bot,
    cotb,
    mbuf,
    mpad,
    ocean_v,
    taps,
    w_in_ref,
    w_out_ref,
    wx,
    xs,
    acc,
    hid,
    slope_v,
    act,
    gh,
    normed,
    gmix,
    gb,
    g_top,
    g_bot,
    gf,
    rstd_v,
    mixed_v,
    out_v,
    igrad_v,
    bsum,
    chan,
    part,
    r1,
    r2,
    r3,
    whole,
    sm,
    s1,
    s2,
    s3,
    s5,
    s6,
    in_send,
    in_recv,
    in_local,
    back_send,
    back_recv,
    back_local,
    w_local,
    halo_send,
    halo_recv,
    send_sem,
    recv_sem,
    z_send,
    z_recv,
):
    H, Wp, C = x_ref.shape
    W = mbuf.shape[1]
    B = Wp // 8
    HID = w_in_ref.shape[1]
    U = Wp // 16
    ends = [(U * k + 3) // 4 * 16 for k in range(5)]
    chunks = list(zip(ends[:-1], ends[1:]))
    inner = [0] + [e + 16 for e in ends[1:-1]] + [Wp - 16]
    segs = [(Wp - 16, Wp)] + list(zip(inner[:-1], inner[1:]))
    m = n // 2
    g = lax.axis_index("group")
    t = lax.axis_index("tile")
    d = lax.axis_index("draw")
    zz = t // 2
    yy = lax.rem(t, 2)
    ty = t + 1 - 2 * yy
    core = (g, t, 1 - d)
    beside = (g, ty, d)
    diag = (g, ty, 1 - d)
    home = yy == d
    away = yy != d
    v = 2 * zz + d

    def at_row(block):
        return (g, 2 * (block // 2) + yy, lax.rem(block, 2))

    up = at_row(lax.rem(v + n - 1, n))
    down = at_row(lax.rem(v + 1, n))
    zpeer = [(g, 2 * lax.rem(zz + k, m) + yy, d) for k in range(m)]

    def remote(src, dst, ss, rs, dev):
        return pltpu.make_async_remote_copy(
            src_ref=src,
            dst_ref=dst,
            send_sem=ss,
            recv_sem=rs,
            device_id=dev,
            device_id_type=pl.DeviceIdType.MESH,
        )

    def moved(src, dst, k):
        return remote(src, dst, in_send.at[k], in_recv.at[k], diag)

    def kept(src, dst, k):
        return pltpu.make_async_copy(src, dst, in_local.at[k])

    load_w = [
        pltpu.make_async_copy(w_in_hbm, w_in_ref, w_local.at[0]),
        pltpu.make_async_copy(w_out_hbm, w_out_ref, w_local.at[1]),
    ]

    def seg(ref, k):
        lo, hi = segs[k]
        return ref.at[:, lo:hi]

    def chunk(ref, k):
        lo, hi = chunks[k]
        return ref.at[:, lo:hi]

    N = len(segs)
    K = len(chunks)

    def x_args(k):
        return seg(x_ref, k), seg(xo, k), k

    def cot_args(k):
        return chunk(cot_ref, k), chunk(cotb, k), N + k

    mask_args = (mask_ref, mbuf, N + K)

    @pl.when(home)
    def _():
        for k in range(N):
            kept(*x_args(k)).start()
        kept(*mask_args).start()

    for copy in load_w:
        copy.start()
    barrier = pltpu.get_barrier_semaphore()
    for dev in [core, beside, diag, up, down] + zpeer[1:]:
        pl.semaphore_signal(barrier, inc=1, device_id=dev, device_id_type=pl.DeviceIdType.MESH)
    pl.semaphore_wait(barrier, m + 4)

    @pl.when(away)
    def _():
        for k in range(N):
            moved(*x_args(k)).start()
        moved(*mask_args).start()

    @pl.when(home)
    def _():
        for k in range(K):
            kept(*cot_args(k)).start()

    for k in range(49):
        taps[k] = jnp.broadcast_to(kern_ref[k // 7, k % 7 : k % 7 + 1, :], (8, C))

    @pl.when(v == 0)
    def _():
        x_top[...] = jnp.zeros_like(x_top)
        g_top[...] = jnp.zeros_like(g_top)

    @pl.when(v == n - 1)
    def _():
        x_bot[...] = jnp.zeros_like(x_bot)
        g_bot[...] = jnp.zeros_like(g_bot)

    def to_up(own, bot, span, k):
        lo, hi = span
        return remote(
            own.at[0:3, lo:hi], bot.at[:, lo:hi], halo_send.at[2 * k], halo_recv.at[2 * k], up
        )

    def to_down(own, top, span, k):
        lo, hi = span
        k = 2 * k + 1
        return remote(
            own.at[H - 3 : H, lo:hi], top.at[:, lo:hi], halo_send.at[k], halo_recv.at[k], down
        )

    def halo_start(own, top, bot, span, k):
        @pl.when(v > 0)
        def _():
            to_up(own, bot, span, k).start()

        @pl.when(v < n - 1)
        def _():
            to_down(own, top, span, k).start()

    def halo_arrive(own, top, bot, span, k):
        @pl.when(v > 0)
        def _():
            to_down(own, top, span, k).wait_recv()

        @pl.when(v < n - 1)
        def _():
            to_up(own, bot, span, k).wait_recv()

    def halo_sent(own, top, bot, span, k):
        @pl.when(v > 0)
        def _():
            to_up(own, bot, span, k).wait_send()

        @pl.when(v < n - 1)
        def _():
            to_down(own, top, span, k).wait_send()

    x_side = (xo, x_top, x_bot)
    g_side = (gb, g_top, g_bot)

    def widen(value, first, lo):
        rows, size, _ = value.shape
        wx[first : first + rows, 8 + lo : 8 + lo + size] = value.astype(F32)

    def spread(span):
        lo, hi = span

        @pl.loop(0, H + 6)
        def _(r):
            for j in range(7):
                xs[j, r, lo // 8 : hi // 8] = wx[r, 5 + j + lo : 5 + j + hi].reshape(
                    (hi - lo) // 8, 8, C
                )

    def wrap_left():
        wx[:, 5:8] = wx[:, 5 + W : 8 + W]

    def wrap_right():
        wx[:, 8 + W : 16 + W] = wx[:, 8:16]

    def conv(span, flip):
        for j in range(7):
            column = [taps[(6 - i) * 7 + 6 - j if flip else i * 7 + j][None] for i in range(7)]

            @pl.loop(span[0] // 16, span[1] // 16)
            def _(c):
                q = pl.ds(c * 2, 2)
                sums = [acc[p, q] if j else None for p in range(H)]
                for r in range(H + 6):
                    cells = xs[j, r, q]
                    for p in range(H):
                        i = r - p
                        if 0 <= i < 7:
                            term = cells * column[i]
                            sums[p] = term if sums[p] is None else sums[p] + term
                for p in range(H):
                    acc[p, q] = sums[p]

    def x_seg(k):
        @pl.when(home)
        def _():
            kept(*x_args(k)).wait()

        @pl.when(away)
        def _():
            moved(*x_args(k)).wait_recv()

        halo_start(*x_side, segs[k], k)
        lo, hi = segs[k]
        widen(xo[:, lo:hi], 3, lo)

    def x_halo(k):
        halo_arrive(*x_side, segs[k], k)
        lo, hi = segs[k]
        widen(x_top[:, lo:hi], 0, lo)
        widen(x_bot[:, lo:hi], H + 3, lo)

    def masks():
        @pl.when(home)
        def _():
            kept(*mask_args).wait()

        @pl.when(away)
        def _():
            moved(*mask_args).wait()

        mpad[...] = jnp.zeros_like(mpad)
        mpad[0:H, 0:W] = mbuf[...].astype(F32)
        flags = mpad[...].astype(BF16)
        lines = lax.broadcasted_iota(jnp.int32, (mpad.shape[0], C), 0)
        for p in range(H):
            pick = jnp.where(lines == p, 1.0, 0.0).astype(BF16)
            ocean_v[p] = lax.dot_general(
                flags, pick, (((0,), (0,)), ((), ())), preferred_element_type=F32
            ).astype(BF16)

    def rowsum(value):
        return jnp.sum(value, axis=0, keepdims=True)

    def give_back(src, dst, k):
        return remote(src, dst, back_send.at[k], back_recv.at[k], diag)

    def put(src, dst, k):
        return pltpu.make_async_copy(src, dst, back_local.at[k])

    def returned(src, dst, k):
        @pl.when(home)
        def _():
            put(src, dst, k).start()

        @pl.when(away)
        def _():
            give_back(src, dst, k).start()

    def cells(k):
        lo, hi = chunks[k]
        return slice(H * lo, H * hi)

    def ocean_of(k):
        lo, hi = chunks[k]
        return ocean_v[:, lo:hi].astype(F32).reshape(H * (hi - lo), C)

    def forward(k):
        lo, hi = chunks[k]
        size = H * (hi - lo)
        at = cells(k)
        conv_out = acc[:, lo // 8 : hi // 8].reshape(size, C) + conv_bias_ref[...]
        dev = conv_out - jnp.mean(conv_out, axis=-1, keepdims=True)
        rstd = lax.rsqrt(jnp.mean(dev * dev, axis=-1, keepdims=True) + EPSILON)
        unit = dev * rstd
        rstd_v[at] = jnp.broadcast_to(rstd, (size, 128))
        gf[at] = unit
        normed[at] = (unit * gain_ref[...] + nbias_ref[...]).astype(BF16)
        hid[0:size] = jnp.dot(normed[at], w_in_ref[...], preferred_element_type=F32)

        @pl.loop(0, size // 16)
        def _(c):
            q = pl.ds(pl.multiple_of(c * 16, 16), 16)
            to = pl.ds(pl.multiple_of(H * lo + c * 16, 16), 16)
            h = hid[q] + b_in_ref[...]
            h2 = h * h
            th = jnp.tanh(h * (h2 * (ROOT_TERM * CUBIC) + ROOT_TERM))
            half = 0.5 * th + 0.5
            a = h * half
            act[to] = a.astype(BF16)
            slope_v[to] = half + (a - a * th) * (h2 * (3.0 * CUBIC * ROOT_TERM) + ROOT_TERM)

        mixed = jnp.dot(act[at], w_out_ref[...], preferred_element_type=F32) + b_out_ref[...]
        mixed_v[at] = mixed
        change = (ocean_of(k) * ls_ref[...] * mixed).reshape(H, hi - lo, C)
        out_v[:, lo:hi] = (xo[:, lo:hi].astype(F32) + change).astype(BF16)
        returned(chunk(out_v, k), chunk(out_ref, k), k)

    for k in range(3):
        x_seg(k)
    masks()
    bsum[...] = jnp.zeros_like(bsum)
    chan[...] = jnp.zeros_like(chan)
    for copy in load_w:
        copy.wait()
    x_halo(0)
    wrap_left()
    for k in range(K):
        x_halo(k + 1)
        if k == 0:
            wrap_right()
        spread(chunks[k])
        conv(chunks[k], False)
        forward(k)
        if k == 0:

            @pl.when(away)
            def _():
                for q in range(N):
                    moved(*x_args(q)).wait_send()
                for q in range(K):
                    moved(*cot_args(q)).start()

            for q in range(3, N):
                x_seg(q)

    for k in range(K):

        @pl.when(home)
        def _():
            kept(*cot_args(k)).wait()

        @pl.when(away)
        def _():
            moved(*cot_args(k)).wait()

        lo, hi = chunks[k]
        size = H * (hi - lo)
        value = cotb[:, lo:hi].astype(F32).reshape(size, C)
        masked = ocean_of(k) * value
        grad_mixed = (ls_ref[...] * masked).astype(BF16)
        gmix[cells(k)] = grad_mixed
        chan[3:4] += rowsum(grad_mixed.astype(F32))
        chan[4:5] += rowsum(masked * mixed_v[cells(k)])

    T = part.shape[4]
    L = part.shape[6]
    tiles = 4 * m * T
    per = C // 16

    class Exchange:
        def __init__(self, w):
            self.w = w
            self.s = 4 * w
            self.z = 2 * (m - 1) * w

        def fill(self, tile):
            for k in range(tiles):
                part[self.w, k // (tiles // 2), k // (tiles // 4) % 2, k // T % m, k % T] = tile(
                    k
                ).astype(BF16)
            self.one().start()

        def one(self):
            w, s = self.w, self.s
            return remote(part.at[w, 1 - d], r1.at[w], send_sem.at[s], recv_sem.at[s], core)

        def two(self):
            w, s = self.w, self.s + 1
            return remote(r1.at[w, 1 - yy], r2.at[w], send_sem.at[s], recv_sem.at[s], beside)

        def three(self):
            w = self.w
            return [
                remote(
                    r2.at[w, lax.rem(zz + k, m)],
                    r3.at[w, k - 1],
                    z_send.at[self.z + k - 1],
                    z_recv.at[self.z + k - 1],
                    zpeer[k],
                )
                for k in range(1, m)
            ]

        def four(self):
            mine = whole.at[self.w, d, yy, zz]
            return [
                remote(
                    mine,
                    mine,
                    z_send.at[self.z + m - 2 + k],
                    z_recv.at[self.z + m - 2 + k],
                    zpeer[k],
                )
                for k in range(1, m)
            ]

        def five(self):
            mine = whole.at[self.w, d, yy]
            s = self.s + 2
            return remote(mine, mine, send_sem.at[s], recv_sem.at[s], beside)

        def six(self):
            mine = whole.at[self.w, d]
            s = self.s + 3
            return remote(mine, mine, send_sem.at[s], recv_sem.at[s], core)

        def after_one(self):
            w = self.w
            self.one().wait()
            r1[w] = (part[w, d].astype(F32) + r1[w].astype(F32)).astype(BF16)
            self.two().start()

        def after_two(self):
            w = self.w
            self.two().wait()
            r2[w] = (r1[w, yy].astype(F32) + r2[w].astype(F32)).astype(BF16)
            for copy in self.three():
                copy.start()

        def after_three(self):
            w = self.w
            for copy in self.three():
                copy.wait()
            total = r2[w, zz].astype(F32)
            for k in range(m - 1):
                total = total + r3[w, k].astype(F32)
            whole[w, d, yy, zz] = (total * scale).astype(BF16)
            for copy in self.four():
                copy.start()

        def after_four(self):
            for copy in self.four():
                copy.wait()
            self.five().start()

        def after_five(self):
            self.five().wait()
            self.six().start()

        def after_six(self):
            self.six().wait()

    ex_out = [Exchange(0), Exchange(1)]
    ex_in = [Exchange(2), Exchange(3)]

    d_out = lax.dot_general(
        gmix[...], act[...], (((0,), (0,)), ((), ())), preferred_element_type=F32
    ).T
    for e in range(2):
        ex_out[e].fill(lambda k: d_out[k * 16 : k * 16 + 16, e * L : e * L + L])

    def grads_hidden(k):
        lo, hi = chunks[k]
        size = H * (hi - lo)
        hid[0:size] = lax.dot_general(
            gmix[cells(k)], w_out_ref[...], (((1,), (1,)), ((), ())), preferred_element_type=F32
        )

        @pl.loop(0, size // 16)
        def _(c):
            q = pl.ds(pl.multiple_of(c * 16, 16), 16)
            to = pl.ds(pl.multiple_of(H * lo + c * 16, 16), 16)
            grad_hidden = (hid[q] * slope_v[to]).astype(BF16)
            gh[to] = grad_hidden
            wide = grad_hidden.astype(F32)
            bsum[...] += wide[0:8] + wide[8:16]

    def grads_conv(k):
        lo, hi = chunks[k]
        at = cells(k)
        grad_normed = lax.dot_general(
            gh[at], w_in_ref[...], (((1,), (1,)), ((), ())), preferred_element_type=F32
        )
        unit = gf[at]
        scaled = grad_normed * gain_ref[...]
        grad_conv = rstd_v[at][:, 0:1] * (
            scaled
            - jnp.mean(scaled, axis=-1, keepdims=True)
            - unit * jnp.mean(scaled * unit, axis=-1, keepdims=True)
        )
        rounded = grad_conv.astype(BF16).reshape(H, hi - lo, C)
        gb[:, lo:hi] = rounded
        halo_start(*g_side, chunks[k], N + k)
        wide = rounded.astype(F32)
        widen(wide, 3, lo)
        chan[0:1] += rowsum(wide.reshape(H * (hi - lo), C))
        chan[1:2] += rowsum(grad_normed * unit)
        chan[2:3] += rowsum(grad_normed)

    for k in range(K):
        grads_hidden(k)

    for ex in ex_out:
        ex.after_one()
    d_in = lax.dot_general(
        normed[...], gh[...], (((0,), (0,)), ((), ())), preferred_element_type=F32
    )

    def in_tile(e, k):
        rb, cb = k % per, k // per * C + e * L
        return d_in[rb * 16 : rb * 16 + 16, cb : cb + L]

    for e in range(2):
        ex_in[e].fill(lambda k: in_tile(e, k))
    for k in range(K):
        grads_conv(k)
        if k == 1:
            for ex in ex_in:
                ex.after_one()
    for ex in ex_out:
        ex.after_two()
    ex_in[0].after_two()

    for j in range(7):

        def tap_terms(c, sums):
            q = pl.ds(c * 2, 2)
            cells16 = pl.ds(pl.multiple_of(c * 16, 16), 16)
            grads = [gb[p, cells16].astype(F32).reshape(2, 8, C) for p in range(H)]
            sums = list(sums)
            for r in range(H + 6):
                cells = xs[j, r, q]
                for p in range(H):
                    i = r - p
                    if 0 <= i < 7:
                        term = cells * grads[p]
                        sums[i] = sums[i] + (term[0] + term[1])
            return tuple(sums)

        sums = lax.fori_loop(0, B // 2, tap_terms, tuple(jnp.zeros((8, C), F32) for _ in range(7)))
        for i in range(7):
            k = i * 7 + j
            sm[k // 32, k % 32 : k % 32 + 1] = rowsum(sums[i])
        if j == 1:
            ex_in[1].after_two()
        if j == 3:
            ex_in[0].after_three()
        if j == 4:
            ex_in[1].after_three()
        if j == 5:
            for ex in ex_out:
                ex.after_three()

    hidden_sum = rowsum(bsum[...])
    for k in range(HID // C):
        sm[1, 17 + k : 18 + k] = hidden_sum[:, k * C : k * C + C]
    sm[1, 21:26] = chan[0:5]
    sm[1, 26:32] = jnp.zeros((6, C), F32)

    small1 = remote(sm.at[1 - d], s1, send_sem.at[16], recv_sem.at[16], core)
    small1.start()

    for k in range(K):
        lo, hi = chunks[k]
        halo_arrive(*g_side, chunks[k], N + k)
        widen(g_top[:, lo:hi], 0, lo)
        widen(g_bot[:, lo:hi], H + 3, lo)
    wrap_left()
    wrap_right()
    small1.wait()
    s2[...] = sm[d] + s1[...]
    small2 = remote(s2, s3, send_sem.at[17], recv_sem.at[17], beside)
    small2.start()
    ex_in[0].after_four()

    zs = 8 * (m - 1) - 1

    def small3():
        return [
            remote(s5.at[zz], s5.at[zz], z_send.at[zs + k], z_recv.at[zs + k], zpeer[k])
            for k in range(1, m)
        ]

    for k in range(K):
        lo, hi = chunks[k]
        spread(chunks[k])
        conv(chunks[k], True)
        igrad_v[:, lo:hi] = (
            cotb[:, lo:hi].astype(F32) + acc[:, lo // 8 : hi // 8].reshape(H, hi - lo, C)
        ).astype(BF16)
        returned(chunk(igrad_v, k), chunk(igrad_ref, k), K + k)
        if k == 0:
            ex_in[1].after_four()
            for ex in ex_out:
                ex.after_four()
        if k == 2:
            for ex in ex_in:
                ex.after_five()
            for ex in ex_out:
                ex.after_five()
        if k == 1:
            small2.wait()
            s5[zz] = s2[...] + s3[...]
            for copy in small3():
                copy.start()

    for copy in small3():
        copy.wait()
    small_total = s5[0]
    for k in range(1, m):
        small_total = small_total + s5[k]
    s6[d] = small_total * scale
    small4 = remote(s6.at[d], s6.at[d], send_sem.at[18], recv_sem.at[18], core)
    small4.start()
    for k in range(N):
        halo_sent(*x_side, segs[k], k)
    for k in range(K):
        halo_sent(*g_side, chunks[k], N + k)
    for ex in ex_out:
        ex.after_six()
    last = [pltpu.make_async_copy(whole.at[0:2], wo_ref, w_local.at[0])]
    last[0].start()
    for ex in ex_in:
        ex.after_six()
    last.append(pltpu.make_async_copy(whole.at[2:4], wi_ref, w_local.at[1]))
    last[1].start()
    small4.wait()
    last.append(pltpu.make_async_copy(s6, rows_ref, w_local.at[2]))
    last[2].start()
    for k in range(2 * K):
        src, dst = ((out_v, out_ref), (igrad_v, igrad_ref))[k // K]
        pair = (chunk(src, k % K), chunk(dst, k % K), k)

        @pl.when(home)
        def _():
            put(*pair).wait()

        @pl.when(away)
        def _():
            give_back(*pair).wait()

    for copy in last:
        copy.wait()


def gather_kernel(wi_part, wo_part, rows_part, wi_ref, wo_ref, kgrad_ref, bgrad_ref, chan_ref):
    C = wi_ref.shape[0]
    HID = wi_ref.shape[1]
    per = C // 16
    _, _, _, m, T, _, L = wi_part.shape
    tiles = 4 * m * T
    rows = rows_part[...].reshape(64, C)
    for i in range(7):
        kgrad_ref[i] = rows[i * 7 : i * 7 + 7]
    for k in range(HID // C):
        bgrad_ref[0:1, k * C : k * C + C] = rows[49 + k : 50 + k]
    chan_ref[...] = rows[49 + HID // C : 54 + HID // C]
    for k in range(tiles):
        at = (k // (tiles // 2), k // (tiles // 4) % 2, k // T % m, k % T)
        rb, cb = k % per, k // per
        for e in range(2):
            wi_ref[rb * 16 : rb * 16 + 16, cb * C + e * L : cb * C + e * L + L] = wi_part[
                (e,) + at
            ].astype(F32)
            wo_ref[k * 16 : k * 16 + 16, e * L : e * L + L] = wo_part[(e,) + at].astype(F32)


def per_device(
    n,
    draws,
    inputs,
    land_mask,
    kernel,
    conv_bias,
    norm_gain,
    norm_bias,
    w_in,
    b_in,
    w_out,
    b_out,
    layer_scale,
    cotangent,
):
    _, H, W, C = inputs.shape
    HID = w_in.shape[1]
    Wp = (W + 15) // 16 * 16
    B = Wp // 8
    m = n // 2
    T = HID // 16 // (2 * n)
    scale = float(1.0 / (draws * H * n * W) ** 0.5)
    vm = pl.BlockSpec(memory_space=pltpu.VMEM)
    hbm = pl.BlockSpec(memory_space=pl.ANY)
    flat = H * Wp
    L = C // 2
    scratch = [
        ((H, Wp, C), BF16),
        ((3, Wp, C), BF16),
        ((3, Wp, C), BF16),
        ((H, Wp, C), BF16),
        ((H, W), jnp.int32),
        ((16, Wp), F32),
        ((H, Wp, C), BF16),
        ((49, 8, C), F32),
        ((C, HID), BF16),
        ((HID, C), BF16),
        ((H + 6, Wp + 16, C), F32),
        ((7, H + 6, B, 8, C), F32),
        ((H, B, 8, C), F32),
        ((flat // 4 + 256, HID), F32),
        ((flat, HID), F32),
        ((flat, HID), BF16),
        ((flat, HID), BF16),
        ((flat, C), BF16),
        ((flat, C), BF16),
        ((H, Wp, C), BF16),
        ((3, Wp, C), BF16),
        ((3, Wp, C), BF16),
        ((flat, C), F32),
        ((flat, 128), F32),
        ((flat, C), F32),
        ((H, Wp, C), BF16),
        ((H, Wp, C), BF16),
        ((8, HID), F32),
        ((8, C), F32),
        ((4, 2, 2, m, T, 16, L), BF16),
        ((4, 2, m, T, 16, L), BF16),
        ((4, m, T, 16, L), BF16),
        ((4, m - 1, T, 16, L), BF16),
        ((4, 2, 2, m, T, 16, L), BF16),
        ((2, 32, C), F32),
        ((32, C), F32),
        ((32, C), F32),
        ((32, C), F32),
        ((m, 32, C), F32),
        ((2, 32, C), F32),
    ]
    dma = pltpu.SemaphoreType.DMA
    output, input_grad, wi_part, wo_part, rows_part = pl.pallas_call(
        functools.partial(block_kernel, n, scale),
        out_shape=(
            jax.ShapeDtypeStruct((H, Wp, C), BF16),
            jax.ShapeDtypeStruct((H, Wp, C), BF16),
            jax.ShapeDtypeStruct((2, 2, 2, m, T, 16, L), BF16),
            jax.ShapeDtypeStruct((2, 2, 2, m, T, 16, L), BF16),
            jax.ShapeDtypeStruct((2, 32, C), F32),
        ),
        in_specs=[hbm, hbm, hbm, vm, vm, vm, vm, hbm, vm, hbm, vm, vm],
        out_specs=[hbm] * 5,
        scratch_shapes=[pltpu.VMEM(shape, dtype) for shape, dtype in scratch]
        + [
            dma((10,)),
            dma((10,)),
            dma((10,)),
            dma((8,)),
            dma((8,)),
            dma((8,)),
            dma((3,)),
            dma((18,)),
            dma((18,)),
            dma((19,)),
            dma((19,)),
            dma((9 * (m - 1),)),
            dma((9 * (m - 1),)),
        ],
        compiler_params=pltpu.CompilerParams(
            collective_id=0, has_side_effects=True, vmem_limit_bytes=60 * 1024 * 1024
        ),
        name="block",
    )(
        jnp.concatenate([inputs[0], inputs[0, :, : Wp - W]], axis=1),
        jnp.concatenate([cotangent[0], cotangent[0, :, : Wp - W]], axis=1),
        land_mask,
        kernel,
        conv_bias[None],
        norm_gain[None],
        norm_bias[None],
        w_in,
        b_in[None],
        w_out,
        b_out[None],
        layer_scale[None],
    )
    w_in_grad, w_out_grad, kernel_grad, b_in_grad, channel = pl.pallas_call(
        gather_kernel,
        out_shape=(
            jax.ShapeDtypeStruct((C, HID), F32),
            jax.ShapeDtypeStruct((HID, C), F32),
            jax.ShapeDtypeStruct((7, 7, C), F32),
            jax.ShapeDtypeStruct((1, HID), F32),
            jax.ShapeDtypeStruct((5, C), F32),
        ),
        in_specs=[vm] * 3,
        out_specs=[vm] * 5,
        name="gather",
    )(wi_part, wo_part, rows_part)
    return (
        output[None, :, 0:W],
        input_grad[None, :, 0:W],
        kernel_grad,
        w_in_grad,
        w_out_grad,
        b_in_grad[0],
        channel,
    )


def solution(mesh):
    field = P(("group", "draw"), "tile", None, None)
    placed = (field, P("tile", None)) + (P(),) * 9 + (field,)
    return jax.shard_map(
        functools.partial(per_device, mesh.shape["tile"], mesh.shape["draw"]),
        mesh=mesh,
        in_specs=placed,
        out_specs=(
            field,
            field,
            P("group", None, None),
            P("group", None),
            P("group", None),
            P("group"),
            P("group", None),
        ),
        check_vma=False,
    )
```
